256 devices in a mesh: dp: 32 (over x_hi, z, core), tensor: 8 (over y, x_lo).
Axes of the slice: x: 4 (x_hi: 2, x_lo: 2; x = x_hi * 2 + x_lo), y: 4, z: 8, core: 2. Of those that a mesh axis runs over, the one named last changes fastest.
Arguments:
- layer_input: bfloat16 [24576, 5120], P('dp', 'tensor'), may hold values from -6 to 6
- queries: bfloat16 [24576, 5120], P('dp', 'tensor'), may hold values from -160 to 160
- projected_key_value: bfloat16 [24576, 8, 256], P('dp', 'tensor'), may hold values from -6 to 6
- output_grad: bfloat16 [24576, 5120], P('dp', 'tensor'), may hold values from -6 to 6
- projection: bfloat16 [5120, 8, 256], P(None, 'tensor'), may hold values from -0.078125 to 0.078125
- moment: bfloat16 [32, 5120, 8, 256], P('dp', None, 'tensor'), may hold values from -6 to 6
- rewards: float32 [64], P('dp'), may hold values from -16 to 16
- groups: int32 [64], P('dp'), may hold values from 0 to 7, as said below
- lengths: int32 [64], replicated, may hold values from 1 to 384, 8192 in all
- assignment: int32 [64], replicated, may hold values from 0 to 31, as said below
- sync_flags: int32 [8], replicated, may hold values from 0 to 1, as said below
Outputs:
- query_grad: bfloat16 [24576, 5120], P('dp', 'tensor')
- input_grad: bfloat16 [24576, 5120], P('dp', 'tensor')
- moment_out: bfloat16 [32, 5120, 8, 256], P('dp', None, 'tensor')
The draws below stay inside these ranges and needn't reach their ends.
Inputs may be any that keep to these rules, and one draw needn't show every extreme that they name: The lengths add up to 8192 and the longest is exactly 384. `groups`: each prompt has exactly 8 responses. `assignment`: response r goes to replica r // 2 or to replica (r // 2 + 32 // 2) % 32; exactly 1 of the responses of every replica go to the second. `sync_flags`: exactly 4 of the flags are 1.
All inputs are finite; a program needn't handle non-finite values.
Results may differ from the reference program's by a relative error of at most 0.017.
Values may be sent and summed in bfloat16 or wider, within the bound.
A program may use at most 128 MiB of HBM per device.

```python
import math
import jax
import jax.numpy as jnp
import numpy as np
from jax import lax

MODEL_WIDTH = 5120
QUERY_HEADS = 40
KEY_VALUE_HEADS = 8
HEAD_SIZE = 128
LOCAL_RESPONSES = 2
RESPONSE_LENGTH = 384
GROUP = 8
NSYNC = 8
REPLICA_COUNT = 32
RESPONSE_COUNT = 64
TOKEN_SLOTS = 24576
NGROUP = 8
LOCAL_KV_HEADS = 1


def key_base(key, upper_length):
    return jnp.clip(jax.random.normal(key, (TOKEN_SLOTS, KEY_VALUE_HEADS, HEAD_SIZE), jnp.float32), -upper_length, upper_length)


def draw_projected_key_value(key, part):
    offset_start = key_base(key, 5.9)
    key = jax.random.fold_in(key, 11)
    value_vectors = jnp.clip(jax.random.normal(key, (TOKEN_SLOTS, KEY_VALUE_HEADS, HEAD_SIZE), jnp.float32), -6.0, 6.0)
    return jnp.concatenate([offset_start, value_vectors], axis=-1).astype(jnp.bfloat16)


def draw_queries(key, part):
    key = jax.random.fold_in(key, 12)
    fresh = jnp.clip(jax.random.normal(key, (TOKEN_SLOTS, QUERY_HEADS * HEAD_SIZE), jnp.float32), -6.0, 6.0)
    return fresh.astype(jnp.bfloat16)


def draw_rewards(key, part):
    key = jax.random.fold_in(key, 13)
    rising = 1.0 + 2.0 * jnp.arange(RESPONSE_COUNT, dtype=jnp.float32) / (RESPONSE_COUNT - 1)
    return jnp.clip(jax.random.normal(key, (RESPONSE_COUNT,), jnp.float32), -4.0, 4.0) * rising


def draw_groups(key, part):
    key = jax.random.fold_in(key, 14)
    return (jax.random.permutation(key, RESPONSE_COUNT) // GROUP).astype(jnp.int32)


def draw_assignment(key, part):
    key = jax.random.fold_in(key, 15)
    ranks = jax.vmap(lambda single: jax.random.permutation(single, LOCAL_RESPONSES))(jax.random.split(key, REPLICA_COUNT))
    owners = jnp.arange(REPLICA_COUNT, dtype=jnp.int32)[:, None]
    partners = (owners + REPLICA_COUNT // 2) % REPLICA_COUNT
    return jnp.where(ranks < LOCAL_RESPONSES // 2, partners, owners).reshape(RESPONSE_COUNT).astype(jnp.int32)


def draw_sync_flags(key, part):
    key = jax.random.fold_in(key, 16)
    return (jax.random.permutation(key, NSYNC) < NSYNC // 2).astype(jnp.int32)


def draw_moment(key, part):
    key = jax.random.fold_in(key, 17)
    common_moment = jax.random.normal(jax.random.fold_in(key, 1), (1, MODEL_WIDTH, KEY_VALUE_HEADS, 2 * HEAD_SIZE), jnp.float32)
    spread = 0.5
    local_portion = jax.random.normal(jax.random.fold_in(key, 2), (REPLICA_COUNT, MODEL_WIDTH, KEY_VALUE_HEADS, 2 * HEAD_SIZE), jnp.float32)
    return jnp.clip(common_moment + spread * local_portion, -6.0, 6.0).astype(jnp.bfloat16)


def level_of(own_key, extent, cuts, low, top_value):
    factor_of, own = 1.0, jax.random.fold_in(own_key, 6)
    for dim, shards_of in cuts:
        heights = jnp.exp(jax.random.uniform(jax.random.fold_in(own, dim), (shards_of,), jnp.float32, low / len(cuts), top_value / len(cuts)))
        factor_of = factor_of * jnp.repeat(heights, extent[dim] // shards_of).reshape([-1 if axis == dim else 1 for axis in range(len(extent))])
    return factor_of


def split_up(number_of, total, bound, skew):
    loads = [(1 << 20) // math.isqrt(rank ** skew) + 1 for rank in range(2, number_of + 1)]
    spare, holding = total - bound - (number_of - 1), [1] * (number_of - 1)
    while spare > 0:
        candidates = [i for i in range(number_of - 1) if holding[i] < bound]
        whole, remaining = sum([loads[i] for i in candidates]), spare
        for i in candidates:
            more = min(bound - holding[i], max(1, remaining * loads[i] // whole), spare)
            holding[i] = holding[i] + more
            spare = spare - more
    return np.array([bound] + holding)


def ragged(key, count, total, limit, lean):
    if count == 2:
        one = jax.random.randint(key, (), max(1, total - limit), min(limit, total - 1) + 1)
        return jnp.stack([one, total - one])
    sizes = jnp.asarray(split_up(count, total, limit, lean), jnp.int32)
    couples = (count - 1) // 2
    source_of, taker = sizes[1:1 + 2 * couples:2], sizes[2:2 + 2 * couples:2]
    slack = jnp.minimum(source_of - 1, limit - taker)
    passed = jax.random.randint(jax.random.fold_in(key, 1), (couples,), 0, 1 << 20) % (slack + 1)
    sizes = sizes.at[1:1 + 2 * couples:2].set(source_of - passed).at[2:2 + 2 * couples:2].set(taker + passed)
    return sizes[jax.random.permutation(jax.random.fold_in(key, 2), count)]


def gaussian(key, extent, scale, most, pieces=(), held_as=jnp.bfloat16):
    values = jax.random.normal(key, extent, jnp.float32) * scale
    if len(pieces) > 0:
        values = level_of(key, extent, pieces, -0.22, 0.18) * values
    return jnp.clip(values, min=-most, max=most).astype(held_as)


def setup_inputs(seed: int = 0) -> dict:
    streams_of = jax.random.split(jax.random.key(seed), 12)
    layer_input = gaussian(streams_of[0], (TOKEN_SLOTS, MODEL_WIDTH), 1.0, 6.0, ((0, 32), (1, 8)))
    queries = draw_queries(jax.random.fold_in(streams_of[11], 71), 0)
    projected_key_value = draw_projected_key_value(jax.random.fold_in(streams_of[11], 71), 0)
    output_grad = gaussian(streams_of[3], (TOKEN_SLOTS, QUERY_HEADS * HEAD_SIZE), 1.0, 6.0, ((0, 32), (1, 8)))
    projection = gaussian(streams_of[4], (MODEL_WIDTH, KEY_VALUE_HEADS, 2 * HEAD_SIZE), MODEL_WIDTH ** -0.5, 0.078125, ((1, 8),))
    moment = draw_moment(jax.random.fold_in(streams_of[11], 71), 0)
    rewards = draw_rewards(jax.random.fold_in(streams_of[11], 71), 0)
    groups = draw_groups(jax.random.fold_in(streams_of[11], 71), 0)
    lengths = ragged(streams_of[8], RESPONSE_COUNT, RESPONSE_COUNT * RESPONSE_LENGTH // 3, RESPONSE_LENGTH, 2).astype(jnp.int32)
    assignment = draw_assignment(jax.random.fold_in(streams_of[11], 71), 0)
    sync_flags = draw_sync_flags(jax.random.fold_in(streams_of[11], 71), 0)
    return dict(layer_input=layer_input, queries=queries, projected_key_value=projected_key_value, output_grad=output_grad, projection=projection, moment=moment, rewards=rewards, groups=groups, lengths=lengths, assignment=assignment, sync_flags=sync_flags)


def response_grads(queries, projected_key_value, gradient_scaled, length):
    reshaped_query = queries.astype(jnp.float32).reshape(RESPONSE_LENGTH, KEY_VALUE_HEADS, QUERY_HEADS // KEY_VALUE_HEADS, HEAD_SIZE)
    reshaped_gradient = gradient_scaled.astype(jnp.float32).reshape(RESPONSE_LENGTH, KEY_VALUE_HEADS, QUERY_HEADS // KEY_VALUE_HEADS, HEAD_SIZE)
    key_rows = projected_key_value[:, :, :HEAD_SIZE].astype(jnp.float32)
    value_rows = projected_key_value[:, :, HEAD_SIZE:].astype(jnp.float32)
    score_scale = 1.0 / math.sqrt(HEAD_SIZE)
    scores = jnp.einsum('tgjd,sgd->gjts', reshaped_query, key_rows) * score_scale
    position = jnp.arange(RESPONSE_LENGTH)
    allowed = (position[None, :] <= position[:, None]) & (position[None, :] < length)
    scores = jnp.where(allowed, scores, -jnp.inf)
    attention = jnp.exp(scores - lax.optimization_barrier(jnp.max(scores, axis=-1, keepdims=True)))
    attention = attention / lax.optimization_barrier(jnp.sum(attention, axis=-1, keepdims=True))
    value_scores = jnp.einsum('tgjd,sgd->gjts', reshaped_gradient, value_rows)
    row_delta = lax.optimization_barrier(jnp.sum(attention * value_scores, axis=-1, keepdims=True))
    score_grads = lax.optimization_barrier((attention * (value_scores - row_delta)).astype(jnp.bfloat16)).astype(jnp.float32)
    rounded = lax.optimization_barrier(attention.astype(jnp.bfloat16)).astype(jnp.float32)
    query_gradient = (jnp.einsum('gjts,sgd->tgjd', score_grads, key_rows) * score_scale).astype(jnp.bfloat16)
    grad_key = (jnp.einsum('gjts,tgjd->sgd', score_grads, reshaped_query) * score_scale).astype(jnp.bfloat16)
    grad_value = jnp.einsum('gjts,tgjd->sgd', rounded, reshaped_gradient).astype(jnp.bfloat16)
    return (query_gradient.reshape(RESPONSE_LENGTH, QUERY_HEADS * HEAD_SIZE), jnp.concatenate([grad_key, grad_value], axis=-1))

def reference(layer_input, queries, projected_key_value, output_grad, projection, moment, rewards, groups, lengths, assignment, sync_flags):
    group_mean = jax.ops.segment_sum(rewards, groups, num_segments=NGROUP) / GROUP
    advantage = rewards - group_mean[groups]
    live_rows = jnp.arange(RESPONSE_LENGTH)[None, :] < lengths[:, None]
    scaled = advantage[:, None, None] * output_grad.reshape(RESPONSE_COUNT, RESPONSE_LENGTH, QUERY_HEADS * HEAD_SIZE).astype(jnp.float32)
    gradient_scaled = jnp.where(live_rows[:, :, None], scaled, 0.0).astype(jnp.bfloat16)

    def single_response(packed):
        return response_grads(packed[0], packed[1], packed[2], packed[3])
    query_gradient, key_value_gradient = lax.map(single_response, (queries.reshape(RESPONSE_COUNT, RESPONSE_LENGTH, QUERY_HEADS * HEAD_SIZE), projected_key_value.reshape(RESPONSE_COUNT, RESPONSE_LENGTH, KEY_VALUE_HEADS, 2 * HEAD_SIZE), gradient_scaled, lengths))

    def input_rows(pair_rows):
        carried_state = jnp.zeros((RESPONSE_LENGTH, MODEL_WIDTH), jnp.float32)
        for tensor_index in range(KEY_VALUE_HEADS // LOCAL_KV_HEADS):
            first_head = tensor_index * LOCAL_KV_HEADS
            piece_rows = pair_rows[:, first_head:first_head + LOCAL_KV_HEADS].reshape(RESPONSE_LENGTH, LOCAL_KV_HEADS * 2 * HEAD_SIZE)
            weight_rows = projection[:, first_head:first_head + LOCAL_KV_HEADS].reshape(MODEL_WIDTH, LOCAL_KV_HEADS * 2 * HEAD_SIZE)
            term_rows = jnp.dot(piece_rows, weight_rows.T, preferred_element_type=jnp.float32)
            carried_state = carried_state + lax.optimization_barrier(term_rows.astype(jnp.bfloat16)).astype(jnp.float32)
        return carried_state.astype(jnp.bfloat16)
    input_grad = lax.map(input_rows, key_value_gradient).reshape(TOKEN_SLOTS, MODEL_WIDTH)
    slot_inputs = layer_input.reshape(RESPONSE_COUNT, RESPONSE_LENGTH, MODEL_WIDTH)
    token_slot_gradient = key_value_gradient.reshape(RESPONSE_COUNT, RESPONSE_LENGTH, KEY_VALUE_HEADS * 2 * HEAD_SIZE)

    def replica_update(carried_state, replica_number):
        selected_rows = jnp.argsort((assignment != replica_number).astype(jnp.int32), stable=True)[:LOCAL_RESPONSES]
        chosen_inputs = slot_inputs[selected_rows].reshape(LOCAL_RESPONSES * RESPONSE_LENGTH, MODEL_WIDTH)
        selected_gradient = token_slot_gradient[selected_rows].reshape(LOCAL_RESPONSES * RESPONSE_LENGTH, KEY_VALUE_HEADS * 2 * HEAD_SIZE)
        weight_gradient = jnp.dot(chosen_inputs.T, selected_gradient, preferred_element_type=jnp.float32)
        updated_state = (0.9 * moment[replica_number].astype(jnp.float32) + 0.1 * weight_gradient.reshape(MODEL_WIDTH, KEY_VALUE_HEADS, 2 * HEAD_SIZE)).astype(jnp.bfloat16)
        return (carried_state + lax.optimization_barrier(updated_state).astype(jnp.float32), updated_state)
    carried_state, moment_state = lax.scan(replica_update, jnp.zeros((MODEL_WIDTH, KEY_VALUE_HEADS, 2 * HEAD_SIZE), jnp.float32), jnp.arange(REPLICA_COUNT, dtype=jnp.int32))
    mean_state = (carried_state / REPLICA_COUNT).astype(jnp.bfloat16)
    synced_rows = jnp.repeat(sync_flags == 1, MODEL_WIDTH // NSYNC)
    moment_out = jnp.where(synced_rows[None, :, None, None], mean_state[None], moment_state)
    return (query_gradient.reshape(TOKEN_SLOTS, QUERY_HEADS * HEAD_SIZE), input_grad, moment_out)
```

```python
import functools
import math

import jax
import jax.numpy as jnp
from jax import lax
from jax.experimental import pallas as pl
from jax.experimental.pallas import tpu as pltpu
from jax.sharding import PartitionSpec as P

HEAD = 128
HEADS = 5
TENSOR = 8
ZS = 8
REPLICAS = 32
SLOTS = 384
WIDTH = 640
GROUP = 8
SYNCED = 4
CHUNKS = ((0, 640),)
SEMS = 128
BF = jnp.bfloat16
F32 = jnp.float32
MESH = pl.DeviceIdType.MESH


def dot(a, b, ca, cb):
    return lax.dot_general(a, b, (((ca,), (cb,)), ((), ())), preferred_element_type=F32)


def kernel(*refs):
    nc = len(CHUNKS)
    refs = list(refs)
    take = lambda n: [refs.pop(0) for _ in range(n)]
    x_hbm, q_hbm, kv_hbm, do_hbm, proj_hbm, mom_hbm = take(6)
    rewards, groups, lengths, assignment, flags = take(5)
    dq_out, ig_out, mom_out = take(3)
    xv, qv, kvv, dov, pv, pg, mv, xg, xm, kvown, kvg, kva, kvm, st, dqf, dkv = take(16)
    rt = take(1)[0]
    ar = [dict(zip(("sc", "cr", "ab", "zr", "xs", "xr", "mn"), take(7))) for _ in range(nc)]
    ss, rs, ls = take(3)

    dp = lax.axis_index("dp")
    t = lax.axis_index("tensor")
    xh, z, core = dp // 16, lax.rem(dp // 2, ZS), lax.rem(dp, 2)
    y, xl = t // 2, lax.rem(t, 2)

    def dev(xh_=xh, z_=z, core_=core, t_=t):
        return (xh_ * 16 + z_ * 2 + core_, t_)

    def ring(a, i, n):
        return lax.rem(a + (i + n), n)

    yt = lambda i, xl_=xl: ring(y, i, 4) * 2 + xl_
    pair_t = y * 2 + (1 - xl)
    pair = dev(t_=pair_t)
    yp, ym = dev(t_=yt(1)), dev(t_=yt(-1))
    sibling = dev(core_=1 - core)
    partner = dev(xh_=1 - xh)
    across = dev(xh_=1 - xh, t_=pair_t)
    tpeer = [dev(t_=ring(t, i, TENSOR)) for i in range(1, TENSOR)]
    zpeer = [dev(z_=ring(z, i, ZS)) for i in range(1, ZS)]

    counter = [0]
    sent = []

    def xfer(src, there, here, to):
        i = counter[0]
        counter[0] += 1
        copy = pltpu.make_async_remote_copy(src, there, ss.at[i], rs.at[i], device_id=to, device_id_type=MESH)
        copy.start()
        sent.append(copy)
        return pltpu.make_async_remote_copy(src, here, ss.at[i], rs.at[i], device_id=to, device_id_type=MESH)

    def local(src, dst, i):
        copy = pltpu.make_async_copy(src, dst, ls.at[i])
        copy.start()
        return copy

    lx = local(x_hbm, xv, 0)
    lproj = [local(proj_hbm.at[:, :, pl.ds(h * 128, 128)], pv.at[h], 1 + h) for h in range(2)]
    lkv = local(kv_hbm, kvv, 3)
    lq = local(q_hbm, qv, 4)
    ldo = local(do_hbm, dov, 5)
    lmom = local(mom_hbm, mv, 6)

    barrier = pltpu.get_barrier_semaphore()
    others = [sibling, partner, across] + tpeer + zpeer
    for other in others:
        pl.semaphore_signal(barrier, inc=1, device_id=other, device_id_type=MESH)

    moving = [assignment[2 * dp + j] != dp for j in range(2)]
    gone = jnp.where(moving[0], 0, 1)
    kept = 1 - gone

    group_row = lax.broadcasted_iota(jnp.int32, (8, 128), 0)
    tile = jnp.zeros((8, 128), F32)
    for j in range(2):
        tile = tile + jnp.where(group_row == groups[j], rewards[j], 0.0)
    rt[0] = tile

    lx.wait()
    xm[...] = xv[gone]
    xg[t, 0] = xv[kept]
    pl.semaphore_wait(barrier, len(others))

    HALF = SLOTS // 2
    top, low = pl.ds(0, HALF), pl.ds(HALF, HALF)

    def gather_kept(c0, cw):
        cols = pl.ds(c0, cw)
        at = lambda idx, rows=pl.ds(0, SLOTS): xg.at[idx, 0, rows, cols]
        own = at(t)
        a = xfer(own, own, at(pair_t), pair)
        b = xfer(own, own, at(yt(-1)), yp)
        c = xfer(own, own, at(yt(1)), ym)
        yield
        b.wait_recv()
        f = xfer(at(yt(-1), top), at(yt(-1), top), at(yt(2), top), yp)
        d = xfer(at(yt(-1)), at(yt(-1)), at(yt(-1, 1 - xl)), pair)
        c.wait_recv()
        g = xfer(at(yt(1), low), at(yt(1), low), at(yt(2), low), ym)
        e = xfer(at(yt(1)), at(yt(1)), at(yt(1, 1 - xl)), pair)
        yield
        f.wait_recv()
        g.wait_recv()
        h = xfer(at(yt(2)), at(yt(2)), at(yt(2, 1 - xl)), pair)
        yield
        for r in (a, d, e, h):
            r.wait_recv()

    def gather_moved(c0, cw):
        cols = pl.ds(c0, cw)
        at = lambda idx, rows=pl.ds(0, SLOTS): xg.at[idx, 1, rows, cols]
        a = xfer(xm.at[:, cols], at(t), at(pair_t), across)
        yield
        a.wait_recv()
        b = xfer(at(pair_t), at(pair_t), at(t), pair)
        up = [xfer(at(pair_t), at(pair_t), at(yt(-1, 1 - xl)), yp)]
        down = [xfer(at(pair_t), at(pair_t), at(yt(1, 1 - xl)), ym)]
        yield
        b.wait_recv()
        up.append(xfer(at(t), at(t), at(yt(-1)), yp))
        down.append(xfer(at(t), at(t), at(yt(1)), ym))
        last = []
        for i, x_ in ((0, 1 - xl), (1, xl)):
            yield
            up[i].wait_recv()
            p = at(yt(-1, x_), top)
            last.append(xfer(p, p, at(yt(2, x_), top), yp))
            down[i].wait_recv()
            p = at(yt(1, x_), low)
            last.append(xfer(p, p, at(yt(2, x_), low), ym))
        yield
        for r in last:
            r.wait_recv()

    SH = WIDTH // ZS

    def gather_projection():
        for cp in lproj:
            cp.wait()
        mine = pl.ds(pl.multiple_of(z * SH, 16), SH)
        pg[core, t, mine] = pv[core, t, mine]
        got = []
        for i in range(1, TENSOR):
            to = ring(t, i, TENSOR)
            frm = ring(t, -i, TENSOR)
            got.append(
                xfer(pv.at[core, to, mine], pg.at[core, t, mine], pg.at[core, frm, mine], tpeer[i - 1])
            )
        yield
        for r in got:
            r.wait_recv()
        got = []
        for i in range(1, ZS):
            theirs = pl.ds(pl.multiple_of(ring(z, -i, ZS) * SH, 16), SH)
            block = pg.at[core, :, mine]
            got.append(xfer(block, block, pg.at[core, :, theirs], zpeer[i - 1]))
        yield
        for r in got:
            r.wait_recv()
        a = xfer(pg.at[core], pg.at[core], pg.at[1 - core], sibling)
        yield
        a.wait_recv()

    def sum_rewards():
        a = xfer(rt.at[0], rt.at[1], rt.at[1], sibling)
        yield
        a.wait_recv()
        rt[2] = rt[0] + rt[1]
        got = [xfer(rt.at[2], rt.at[2 + i], rt.at[2 + i], zpeer[i - 1]) for i in range(1, ZS)]
        yield
        for r in got:
            r.wait_recv()
        total = rt[2]
        for i in range(1, ZS):
            total = total + rt[2 + i]
        rt[10] = total
        a = xfer(rt.at[10], rt.at[11], rt.at[11], partner)
        yield
        a.wait_recv()

    def attention(r):
        length = lengths[2 * dp + r]
        srow = lax.broadcasted_iota(jnp.int32, (SLOTS, SLOTS), 0)
        tcol = lax.broadcasted_iota(jnp.int32, (SLOTS, SLOTS), 1)
        allowed = (srow <= tcol) & (srow < length)
        live = lax.broadcasted_iota(jnp.int32, (SLOTS, HEAD), 0) < length
        scale = 1.0 / math.sqrt(HEAD)
        dkv[r] = jnp.zeros((SLOTS, 2 * HEAD), F32)

        @pl.loop(0, HEADS)
        def _(h):
            cols = pl.ds(pl.multiple_of(h * HEAD, HEAD), HEAD)
            q = qv[r, :, cols]
            g = jnp.where(live, dov[r, :, cols].astype(F32), 0.0).astype(BF)
            k = kvv[r, :, 0:HEAD]
            v = kvv[r, :, HEAD : 2 * HEAD]
            s = jnp.where(allowed, dot(k, q, 1, 1) * scale, -1e30)
            e = jnp.exp(s - jnp.max(s, axis=0, keepdims=True))
            att = e * (1.0 / jnp.sum(e, axis=0, keepdims=True))
            w = dot(v, g, 1, 1)
            delta = jnp.sum(att * w, axis=0, keepdims=True)
            ds = (att * (w - delta)).astype(BF)
            dkv[r, :, 0:HEAD] += dot(ds, q, 1, 0) * scale
            dkv[r, :, HEAD : 2 * HEAD] += dot(att.astype(BF), g, 1, 0)
            dqf[r, :, cols] = dot(ds, k, 0, 0) * scale

    def finish_attention():
        total = rt[10] + rt[11]
        for r in range(2):
            mean = jnp.sum(jnp.where(group_row == groups[r], total, 0.0), axis=0, keepdims=True)[:, 0:1] / GROUP
            advantage = rewards[r] - mean
            dq_out[r] = (dqf[r] * advantage).astype(BF)
            kvown[r] = (dkv[r] * advantage).astype(BF)
        kvg[t] = kvown[...]
        kva[0] = kvown[kept]
        kvm[...] = kvown[gone]

    def gather_key_values():
        at = lambda idx, r: kvg.at[idx, r]
        a = xfer(kvg.at[t], kvg.at[t], kvg.at[pair_t], pair)
        up = [xfer(kvg.at[t], kvg.at[t], kvg.at[yt(-1)], yp)]
        down = [xfer(kvg.at[t], kvg.at[t], kvg.at[yt(1)], ym)]
        yield
        a.wait_recv()
        up.append(xfer(kvg.at[pair_t], kvg.at[pair_t], kvg.at[yt(-1, 1 - xl)], yp))
        down.append(xfer(kvg.at[pair_t], kvg.at[pair_t], kvg.at[yt(1, 1 - xl)], ym))
        last = []
        for i, x_ in ((0, xl), (1, 1 - xl)):
            yield
            up[i].wait_recv()
            p = at(yt(-1, x_), 0)
            last.append(xfer(p, p, at(yt(2, x_), 0), yp))
            down[i].wait_recv()
            p = at(yt(1, x_), 1)
            last.append(xfer(p, p, at(yt(2, x_), 1), ym))
        yield
        for r in last:
            r.wait_recv()

    rank, where = [], [jnp.int32(0)] * SYNCED
    seen = jnp.int32(0)
    for j in range(TENSOR):
        on = flags[j] == 1
        rank.append(jnp.minimum(seen, SYNCED - 1))
        for k in range(SYNCED):
            where[k] = jnp.where(on & (seen == k), j, where[k])
        seen = seen + jnp.where(on, 1, 0)

    def new_state(c0, cw):
        @pl.loop(0, TENSOR)
        def _(b):
            grad = dot(xg[b, 0, :, c0 : c0 + cw], kva[0], 0, 0) + dot(xg[b, 1, :, c0 : c0 + cw], kva[1], 0, 0)
            st[b, c0 : c0 + cw] = (0.9 * mv[b, c0 : c0 + cw].astype(F32) + 0.1 * grad).astype(BF)

    def average(c0, cw, sc, cr, ab, zr, xs, xr, mn):
        n = cw // 4
        for k in range(SYNCED):
            sc[k // 2, (k % 2) * cw : (k % 2 + 1) * cw] = st[where[k], c0 : c0 + cw]
        a = xfer(sc.at[1 - core], cr, cr, sibling)
        yield
        a.wait_recv()
        for i in range(ZS):
            rows = slice(i * n, (i + 1) * n)
            ab[i] = (sc[core, rows].astype(F32) + cr[rows].astype(F32)).astype(BF)
        got = [xfer(ab.at[ring(z, i, ZS)], zr.at[i - 1], zr.at[i - 1], zpeer[i - 1]) for i in range(1, ZS)]
        yield
        total = ab[z].astype(F32)
        for i in range(1, ZS):
            got[i - 1].wait_recv()
            total = total + zr[i - 1].astype(F32)
        xs[...] = total.astype(BF)
        a = xfer(xs, xr, xr, partner)
        yield
        a.wait_recv()
        mine = mn.at[core * 2 + z // 4, lax.rem(z, 4)]
        mn[core * 2 + z // 4, lax.rem(z, 4)] = (
            (xs[...].astype(F32) + xr[...].astype(F32)) * (1.0 / REPLICAS)
        ).astype(BF)
        got = []
        for i in range(1, ZS):
            other = ring(z, -i, ZS)
            got.append(xfer(mine, mine, mn.at[core * 2 + other // 4, lax.rem(other, 4)], zpeer[i - 1]))
        yield
        for r in got:
            r.wait_recv()
        half = mn.at[pl.ds(core * 2, 2)]
        a = xfer(half, half, mn.at[pl.ds((1 - core) * 2, 2)], sibling)
        yield
        a.wait_recv()
        for j in range(TENSOR):
            synced = mn[rank[j]].reshape(cw, 2 * HEAD)
            mom_out[j, c0 : c0 + cw] = jnp.where(flags[j] == 1, synced, st[j, c0 : c0 + cw])

    def input_gradient():
        @pl.loop(0, 6)
        def _(i):
            r = i // 3
            rows = pl.ds(pl.multiple_of(lax.rem(i, 3) * 128, 128), 128)
            total = jnp.zeros((128, WIDTH), F32)
            for b in range(TENSOR):
                for h in range(2):
                    total = total + dot(kvg[b, r, rows, h * 128 : (h + 1) * 128], pg[h, b], 1, 1)
            ig_out[r, rows] = total.astype(BF)

    def step(*generators):
        for g in generators:
            next(g, None)

    kept_g = [gather_kept(*c) for c in CHUNKS]
    moved_g = [gather_moved(*c) for c in CHUNKS]
    pro, rew = gather_projection(), sum_rewards()
    step(moved_g[0], kept_g[0], rew, pro)
    lkv.wait()
    lq.wait()
    ldo.wait()
    attention(0)
    step(rew, pro)
    attention(1)
    step(rew)
    step(moved_g[0], kept_g[0], pro)
    step(rew)
    finish_attention()
    swap = xfer(kvm, kva.at[1], kva.at[1], partner)
    step(moved_g[0], kept_g[0])
    step(moved_g[0], kept_g[0])
    step(moved_g[0])
    step(moved_g[0])
    kvs = gather_key_values()
    step(kvs, kvs)
    swap.wait_recv()
    lmom.wait()
    new_state(*CHUNKS[0])
    av = [average(*c, **ar[i]) for i, c in enumerate(CHUNKS)]
    step(av[0], av[0], kvs, pro, av[0], kvs, av[0], kvs, av[0])
    input_gradient()
    step(av[0])
    for copy in sent:
        copy.wait_send()


def shards(
    layer_input,
    queries,
    projected_key_value,
    output_grad,
    projection,
    moment,
    rewards,
    groups,
    lengths,
    assignment,
    sync_flags,
):
    any_spec = pl.BlockSpec(memory_space=pl.ANY)
    smem = pl.BlockSpec(memory_space=pltpu.SMEM)
    vmem = pl.BlockSpec(memory_space=pltpu.VMEM)
    scratch = [
        pltpu.VMEM((2, SLOTS, WIDTH), BF),
        pltpu.VMEM((2, SLOTS, WIDTH), BF),
        pltpu.VMEM((2, SLOTS, 2 * HEAD), BF),
        pltpu.VMEM((2, SLOTS, WIDTH), BF),
        pltpu.VMEM((2, TENSOR, WIDTH, HEAD), BF),
        pltpu.VMEM((2, TENSOR, WIDTH, HEAD), BF),
        pltpu.VMEM((TENSOR, WIDTH, 2 * HEAD), BF),
        pltpu.VMEM((TENSOR, 2, SLOTS, WIDTH), BF),
        pltpu.VMEM((SLOTS, WIDTH), BF),
        pltpu.VMEM((2, SLOTS, 2 * HEAD), BF),
        pltpu.VMEM((TENSOR, 2, SLOTS, 2 * HEAD), BF),
        pltpu.VMEM((2, SLOTS, 2 * HEAD), BF),
        pltpu.VMEM((SLOTS, 2 * HEAD), BF),
        pltpu.VMEM((TENSOR, WIDTH, 2 * HEAD), BF),
        pltpu.VMEM((2, SLOTS, WIDTH), F32),
        pltpu.VMEM((2, SLOTS, 2 * HEAD), F32),
        pltpu.VMEM((12, 8, 128), F32),
    ]
    for _, cw in CHUNKS:
        n = cw // 4
        scratch += [
            pltpu.VMEM((2, 2 * cw, 2 * HEAD), BF),
            pltpu.VMEM((2 * cw, 2 * HEAD), BF),
            pltpu.VMEM((ZS, n, 2 * HEAD), BF),
            pltpu.VMEM((ZS - 1, n, 2 * HEAD), BF),
            pltpu.VMEM((n, 2 * HEAD), BF),
            pltpu.VMEM((n, 2 * HEAD), BF),
            pltpu.VMEM((4, 4, n, 2 * HEAD), BF),
        ]
    scratch += [pltpu.SemaphoreType.DMA((SEMS,)), pltpu.SemaphoreType.DMA((SEMS,)), pltpu.SemaphoreType.DMA((8,))]
    dq, ig, out = pl.pallas_call(
        kernel,
        name="layer_back",
        out_shape=(
            jax.ShapeDtypeStruct((2, SLOTS, WIDTH), BF),
            jax.ShapeDtypeStruct((2, SLOTS, WIDTH), BF),
            jax.ShapeDtypeStruct((TENSOR, WIDTH, 2 * HEAD), BF),
        ),
        in_specs=[any_spec] * 6 + [smem] * 5,
        out_specs=(vmem, vmem, vmem),
        scratch_shapes=scratch,
        compiler_params=pltpu.CompilerParams(
            collective_id=0, has_side_effects=True, vmem_limit_bytes=56 * 2**20
        ),
        cost_estimate=pl.CostEstimate(flops=6 * 10**9, bytes_accessed=16 * 10**6, transcendentals=15 * 10**5),
    )(
        layer_input.reshape(2, SLOTS, WIDTH),
        queries.reshape(2, SLOTS, WIDTH),
        projected_key_value.reshape(2, SLOTS, 2 * HEAD),
        output_grad.reshape(2, SLOTS, WIDTH),
        projection.reshape(TENSOR, WIDTH, 2 * HEAD),
        moment.reshape(TENSOR, WIDTH, 2 * HEAD),
        rewards,
        groups,
        lengths,
        assignment,
        sync_flags,
    )
    return (
        dq.reshape(2 * SLOTS, WIDTH),
        ig.reshape(2 * SLOTS, WIDTH),
        out.reshape(1, TENSOR * WIDTH, 1, 2 * HEAD),
    )


def solution(mesh):
    return jax.shard_map(
        shards,
        mesh=mesh,
        in_specs=(
            P("dp", "tensor"),
            P("dp", "tensor"),
            P("dp", "tensor", None),
            P("dp", "tensor"),
            P(None, "tensor", None),
            P("dp", None, "tensor", None),
            P("dp"),
            P("dp"),
            P(),
            P(),
            P(),
        ),
        out_specs=(P("dp", "tensor"), P("dp", "tensor"), P("dp", None, "tensor", None)),
        check_vma=False,
    )
```

```python
import functools
import math

import jax
import jax.numpy as jnp
from jax import lax
from jax.experimental import pallas as pl
from jax.experimental.pallas import tpu as pltpu
from jax.sharding import PartitionSpec as P

HEAD = 128
HEADS = 5
TENSOR = 8
ZS = 8
REPLICAS = 32
SLOTS = 384
WIDTH = 640
GROUP = 8
SYNCED = 4
CHUNKS = ((0, 384), (384, 256))
SEMS = 160
BF = jnp.bfloat16
F32 = jnp.float32
MESH = pl.DeviceIdType.MESH


def dot(a, b, ca, cb):
    return lax.dot_general(a, b, (((ca,), (cb,)), ((), ())), preferred_element_type=F32)


def kernel(*refs):
    nc = len(CHUNKS)
    refs = list(refs)
    take = lambda n: [refs.pop(0) for _ in range(n)]
    x_hbm, q_hbm, kv_hbm, do_hbm, proj_hbm, mom_hbm = take(6)
    rewards, groups, lengths, assignment, flags = take(5)
    dq_hbm, ig_hbm, mom_hbm_out = take(3)
    xv, qv, kvv, dov, pv, pg, mv, xg, xm, kvown, kvg, kva, kvm, st, dqf, dkv = take(16)
    rt, igf, dq_out, ig_out, mom_out = take(5)
    ar = [dict(zip(("sc", "cr", "ab", "zr", "xs", "xr", "mn"), take(7))) for _ in range(nc)]
    ss, rs, ls = take(3)

    dp = lax.axis_index("dp")
    t = lax.axis_index("tensor")
    xh, z, core = dp // 16, lax.rem(dp // 2, ZS), lax.rem(dp, 2)
    y, xl = t // 2, lax.rem(t, 2)

    def dev(xh_=xh, z_=z, core_=core, t_=t):
        return (xh_ * 16 + z_ * 2 + core_, t_)

    def ring(a, i, n):
        return lax.rem(a + (i + n), n)

    yt = lambda i, xl_=xl: ring(y, i, 4) * 2 + xl_
    pair_t = y * 2 + (1 - xl)
    pair = dev(t_=pair_t)
    yp, ym = dev(t_=yt(1)), dev(t_=yt(-1))
    sibling = dev(core_=1 - core)
    partner = dev(xh_=1 - xh)
    across = dev(xh_=1 - xh, t_=pair_t)
    tpeer = [dev(t_=ring(t, i, TENSOR)) for i in range(1, TENSOR)]
    zpeer = [dev(z_=ring(z, i, ZS)) for i in range(1, ZS)]

    counter = [0]
    sent = []

    def xfer(src, there, here, to):
        i = counter[0]
        counter[0] += 1
        copy = pltpu.make_async_remote_copy(src, there, ss.at[i], rs.at[i], device_id=to, device_id_type=MESH)
        copy.start()
        sent.append(copy)
        return pltpu.make_async_remote_copy(src, here, ss.at[i], rs.at[i], device_id=to, device_id_type=MESH)

    def local(src, dst, i):
        copy = pltpu.make_async_copy(src, dst, ls.at[i])
        copy.start()
        return copy

    lx = local(x_hbm, xv, 0)
    lproj = [local(proj_hbm.at[:, :, pl.ds(h * 128, 128)], pv.at[h], 1 + h) for h in range(2)]
    lkv = local(kv_hbm, kvv, 3)
    lq = local(q_hbm, qv, 4)
    ldo = local(do_hbm, dov, 5)
    lmom = local(mom_hbm, mv, 6)

    barrier = pltpu.get_barrier_semaphore()
    others = [sibling, partner, across] + tpeer + zpeer
    for other in others:
        pl.semaphore_signal(barrier, inc=1, device_id=other, device_id_type=MESH)

    moving = [assignment[2 * dp + j] != dp for j in range(2)]
    gone = jnp.where(moving[0], 0, 1)
    kept = 1 - gone

    group_row = lax.broadcasted_iota(jnp.int32, (8, 128), 0)
    tile = jnp.zeros((8, 128), F32)
    for j in range(2):
        tile = tile + jnp.where(group_row == groups[j], rewards[j], 0.0)
    rt[0] = tile

    lx.wait()
    xm[...] = xv[gone]
    xg[t, 0] = xv[kept]
    pl.semaphore_wait(barrier, len(others))

    HALF = SLOTS // 2
    top, low = pl.ds(0, HALF), pl.ds(HALF, HALF)

    def gather_kept(c0, cw):
        cols = pl.ds(c0, cw)
        at = lambda idx, rows=pl.ds(0, SLOTS): xg.at[idx, 0, rows, cols]
        own = at(t)
        a = xfer(own, own, at(pair_t), pair)
        b = xfer(own, own, at(yt(-1)), yp)
        c = xfer(own, own, at(yt(1)), ym)
        yield
        b.wait_recv()
        f = xfer(at(yt(-1), top), at(yt(-1), top), at(yt(2), top), yp)
        c.wait_recv()
        g = xfer(at(yt(1), low), at(yt(1), low), at(yt(2), low), ym)
        yield
        d = xfer(at(yt(-1)), at(yt(-1)), at(yt(-1, 1 - xl)), pair)
        e = xfer(at(yt(1)), at(yt(1)), at(yt(1, 1 - xl)), pair)
        yield
        f.wait_recv()
        g.wait_recv()
        h = xfer(at(yt(2)), at(yt(2)), at(yt(2, 1 - xl)), pair)
        yield
        for r in (a, d, e):
            r.wait_recv()
        yield
        h.wait_recv()

    def gather_moved(c0, cw):
        cols = pl.ds(c0, cw)
        at = lambda idx, rows=pl.ds(0, SLOTS): xg.at[idx, 1, rows, cols]
        a = xfer(xm.at[:, cols], at(t), at(pair_t), across)
        yield
        a.wait_recv()
        b = xfer(at(pair_t), at(pair_t), at(t), pair)
        up = [xfer(at(pair_t), at(pair_t), at(yt(-1, 1 - xl)), yp)]
        down = [xfer(at(pair_t), at(pair_t), at(yt(1, 1 - xl)), ym)]
        yield
        b.wait_recv()
        up.append(xfer(at(t), at(t), at(yt(-1)), yp))
        down.append(xfer(at(t), at(t), at(yt(1)), ym))
        last = []
        for i, x_ in ((0, 1 - xl), (1, xl)):
            yield
            up[i].wait_recv()
            p = at(yt(-1, x_), top)
            last.append(xfer(p, p, at(yt(2, x_), top), yp))
            down[i].wait_recv()
            p = at(yt(1, x_), low)
            last.append(xfer(p, p, at(yt(2, x_), low), ym))
        yield
        for r in last:
            r.wait_recv()

    SH = WIDTH // ZS

    def gather_projection():
        for cp in lproj:
            cp.wait()
        mine = pl.ds(pl.multiple_of(z * SH, 16), SH)
        pg[core, t, mine] = pv[core, t, mine]
        got = []
        for i in range(1, TENSOR):
            to = ring(t, i, TENSOR)
            frm = ring(t, -i, TENSOR)
            got.append(
                xfer(pv.at[core, to, mine], pg.at[core, t, mine], pg.at[core, frm, mine], tpeer[i - 1])
            )
        yield
        for r in got:
            r.wait_recv()
        got = []
        for i in range(1, ZS):
            theirs = pl.ds(pl.multiple_of(ring(z, -i, ZS) * SH, 16), SH)
            block = pg.at[core, :, mine]
            got.append(xfer(block, block, pg.at[core, :, theirs], zpeer[i - 1]))
        yield
        for r in got:
            r.wait_recv()
        a = xfer(pg.at[core], pg.at[core], pg.at[1 - core], sibling)
        yield
        a.wait_recv()

    def sum_rewards():
        a = xfer(rt.at[0], rt.at[1], rt.at[1], sibling)
        yield
        a.wait_recv()
        rt[2] = rt[0] + rt[1]
        got = [xfer(rt.at[2], rt.at[2 + i], rt.at[2 + i], zpeer[i - 1]) for i in range(1, ZS)]
        yield
        for r in got:
            r.wait_recv()
        total = rt[2]
        for i in range(1, ZS):
            total = total + rt[2 + i]
        rt[10] = total
        a = xfer(rt.at[10], rt.at[11], rt.at[11], partner)
        yield
        a.wait_recv()

    def attention(r):
        length = lengths[2 * dp + r]
        srow = lax.broadcasted_iota(jnp.int32, (SLOTS, SLOTS), 0)
        tcol = lax.broadcasted_iota(jnp.int32, (SLOTS, SLOTS), 1)
        allowed = (srow <= tcol) & (srow < length)
        live = lax.broadcasted_iota(jnp.int32, (SLOTS, HEAD), 0) < length
        scale = 1.0 / math.sqrt(HEAD)
        dkv[r] = jnp.zeros((SLOTS, 2 * HEAD), F32)

        @pl.loop(0, HEADS)
        def _(h):
            cols = pl.ds(pl.multiple_of(h * HEAD, HEAD), HEAD)
            q = qv[r, :, cols]
            g = jnp.where(live, dov[r, :, cols].astype(F32), 0.0).astype(BF)
            k = kvv[r, :, 0:HEAD]
            v = kvv[r, :, HEAD : 2 * HEAD]
            s = jnp.where(allowed, dot(k, q, 1, 1) * scale, -1e30)
            e = jnp.exp(s - jnp.max(s, axis=0, keepdims=True))
            att = e * (1.0 / jnp.sum(e, axis=0, keepdims=True))
            w = dot(v, g, 1, 1)
            delta = jnp.sum(att * w, axis=0, keepdims=True)
            ds = (att * (w - delta)).astype(BF)
            dkv[r, :, 0:HEAD] += dot(ds, q, 1, 0) * scale
            dkv[r, :, HEAD : 2 * HEAD] += dot(att.astype(BF), g, 1, 0)
            dqf[r, :, cols] = dot(ds, k, 0, 0) * scale

    def finish_attention():
        total = rt[10] + rt[11]
        for r in range(2):
            mean = jnp.sum(jnp.where(group_row == groups[r], total, 0.0), axis=0, keepdims=True)[:, 0:1] / GROUP
            advantage = rewards[r] - mean
            dq_out[r] = (dqf[r] * advantage).astype(BF)
            kvown[r] = (dkv[r] * advantage).astype(BF)
        kvg[t] = kvown[...]
        kva[0] = kvown[kept]
        kvm[...] = kvown[gone]

    def gather_key_values():
        at = lambda idx, r: kvg.at[idx, r]
        a = xfer(kvg.at[t], kvg.at[t], kvg.at[pair_t], pair)
        up = [xfer(kvg.at[t], kvg.at[t], kvg.at[yt(-1)], yp)]
        down = [xfer(kvg.at[t], kvg.at[t], kvg.at[yt(1)], ym)]
        yield
        a.wait_recv()
        up.append(xfer(kvg.at[pair_t], kvg.at[pair_t], kvg.at[yt(-1, 1 - xl)], yp))
        down.append(xfer(kvg.at[pair_t], kvg.at[pair_t], kvg.at[yt(1, 1 - xl)], ym))
        last = []
        for i, x_ in ((0, xl), (1, 1 - xl)):
            yield
            up[i].wait_recv()
            p = at(yt(-1, x_), 0)
            last.append(xfer(p, p, at(yt(2, x_), 0), yp))
            down[i].wait_recv()
            p = at(yt(1, x_), 1)
            last.append(xfer(p, p, at(yt(2, x_), 1), ym))
        yield
        for r in last:
            r.wait_recv()

    rank, where = [], [jnp.int32(0)] * SYNCED
    seen = jnp.int32(0)
    for j in range(TENSOR):
        on = flags[j] == 1
        rank.append(jnp.minimum(seen, SYNCED - 1))
        for k in range(SYNCED):
            where[k] = jnp.where(on & (seen == k), j, where[k])
        seen = seen + jnp.where(on, 1, 0)

    def new_state(c0, cw):
        @pl.loop(0, TENSOR)
        def _(b):
            grad = dot(xg[b, 0, :, c0 : c0 + cw], kva[0], 0, 0) + dot(xg[b, 1, :, c0 : c0 + cw], kva[1], 0, 0)
            st[b, c0 : c0 + cw] = (0.9 * mv[b, c0 : c0 + cw].astype(F32) + 0.1 * grad).astype(BF)

    def average(c0, cw, sc, cr, ab, zr, xs, xr, mn):
        n = cw // 4
        for k in range(SYNCED):
            sc[k // 2, (k % 2) * cw : (k % 2 + 1) * cw] = st[where[k], c0 : c0 + cw]
        a = xfer(sc.at[1 - core], cr, cr, sibling)
        yield
        a.wait_recv()
        for i in range(ZS):
            rows = slice(i * n, (i + 1) * n)
            ab[i] = (sc[core, rows].astype(F32) + cr[rows].astype(F32)).astype(BF)
        got = [xfer(ab.at[ring(z, i, ZS)], zr.at[i - 1], zr.at[i - 1], zpeer[i - 1]) for i in range(1, ZS)]
        yield
        total = ab[z].astype(F32)
        for i in range(1, ZS):
            got[i - 1].wait_recv()
            total = total + zr[i - 1].astype(F32)
        xs[...] = total.astype(BF)
        a = xfer(xs, xr, xr, partner)
        yield
        a.wait_recv()
        mine = mn.at[core * 2 + z // 4, lax.rem(z, 4)]
        mn[core * 2 + z // 4, lax.rem(z, 4)] = (
            (xs[...].astype(F32) + xr[...].astype(F32)) * (1.0 / REPLICAS)
        ).astype(BF)
        got = []
        for i in range(1, ZS):
            other = ring(z, -i, ZS)
            got.append(xfer(mine, mine, mn.at[core * 2 + other // 4, lax.rem(other, 4)], zpeer[i - 1]))
        yield
        for r in got:
            r.wait_recv()
        half = mn.at[pl.ds(core * 2, 2)]
        a = xfer(half, half, mn.at[pl.ds((1 - core) * 2, 2)], sibling)
        yield
        a.wait_recv()
        for j in range(TENSOR):
            synced = mn[rank[j]].reshape(cw, 2 * HEAD)
            mom_out[j, c0 : c0 + cw] = jnp.where(flags[j] == 1, synced, st[j, c0 : c0 + cw])

    def input_gradient(blocks, first, last):
        @pl.loop(0, 2)
        def _(r):
            total = None if first else igf[r]
            for b in blocks:
                weight = jnp.concatenate([pg[0, b], pg[1, b]], axis=1)
                term = dot(kvg[b, r], weight, 1, 1)
                total = term if total is None else total + term
            if last:
                ig_out[r] = total.astype(BF)
            else:
                igf[r] = total

    stores = []

    def store(src, dst):
        copy = pltpu.make_async_copy(src, dst, ls.at[7 + len(stores)])
        copy.start()
        stores.append(copy)

    def step(*generators):
        for g in generators:
            next(g, None)

    k0, k1 = [gather_kept(*c) for c in CHUNKS]
    m0, m1 = [gather_moved(*c) for c in CHUNKS]
    a0, a1 = [average(*c, **ar[i]) for i, c in enumerate(CHUNKS)]
    kvs = gather_key_values()
    pro, rew = gather_projection(), sum_rewards()
    step(m0, m1, k0, k1, rew, pro)
    lkv.wait()
    lq.wait()
    ldo.wait()
    attention(0)
    step(rew, pro)
    attention(1)
    step(rew)
    step(m0, m1, k0, k1)
    step(rew)
    finish_attention()
    store(dq_out, dq_hbm)
    swap = xfer(kvm, kva.at[1], kva.at[1], partner)
    step(m0, k0, m1, k0)
    step(pro)
    step(m0, m0, m1, m1)
    step(k0)
    step(k1, k1)
    step(kvs)
    step(k0, m0)
    swap.wait_recv()
    lmom.wait()
    new_state(*CHUNKS[0])
    step(a0, a0)
    step(k1, k1, m1)
    new_state(*CHUNKS[1])
    step(a1, a0, a1)
    step(kvs, pro, a0, kvs, a1, a0, a1, kvs)
    input_gradient((t, pair_t, yt(-1), yt(1), yt(-1, 1 - xl), yt(1, 1 - xl)), True, False)
    step(a0, a1)
    step(kvs)
    input_gradient((yt(2), yt(2, 1 - xl)), False, True)
    store(ig_out, ig_hbm)
    step(a1)
    store(mom_out, mom_hbm_out)
    for copy in stores:
        copy.wait()
    for copy in sent:
        copy.wait_send()


def place(dq, ig, out, dq_to, ig_to, out_to, dq_v, ig_v, out_v, sems):
    parts = [(a.at[r], v.at[r], b.at[r]) for a, v, b in ((dq, dq_v, dq_to), (ig, ig_v, ig_to)) for r in range(2)]
    parts += [(out.at[j], out_v.at[j], out_to.at[j]) for j in range(TENSOR)]
    loads = [pltpu.make_async_copy(a, v, sems.at[0, i]) for i, (a, v, _) in enumerate(parts)]
    stores = [pltpu.make_async_copy(v, b, sems.at[1, i]) for i, (_, v, b) in enumerate(parts)]
    for load in loads:
        load.start()
    for load, store in zip(loads, stores):
        load.wait()
        store.start()
    for store in stores:
        store.wait()


def shards(
    layer_input,
    queries,
    projected_key_value,
    output_grad,
    projection,
    moment,
    rewards,
    groups,
    lengths,
    assignment,
    sync_flags,
):
    any_spec = pl.BlockSpec(memory_space=pl.ANY)
    smem = pl.BlockSpec(memory_space=pltpu.SMEM)
    scratch = [
        pltpu.VMEM((2, SLOTS, WIDTH), BF),
        pltpu.VMEM((2, SLOTS, WIDTH), BF),
        pltpu.VMEM((2, SLOTS, 2 * HEAD), BF),
        pltpu.VMEM((2, SLOTS, WIDTH), BF),
        pltpu.VMEM((2, TENSOR, WIDTH, HEAD), BF),
        pltpu.VMEM((2, TENSOR, WIDTH, HEAD), BF),
        pltpu.VMEM((TENSOR, WIDTH, 2 * HEAD), BF),
        pltpu.VMEM((TENSOR, 2, SLOTS, WIDTH), BF),
        pltpu.VMEM((SLOTS, WIDTH), BF),
        pltpu.VMEM((2, SLOTS, 2 * HEAD), BF),
        pltpu.VMEM((TENSOR, 2, SLOTS, 2 * HEAD), BF),
        pltpu.VMEM((2, SLOTS, 2 * HEAD), BF),
        pltpu.VMEM((SLOTS, 2 * HEAD), BF),
        pltpu.VMEM((TENSOR, WIDTH, 2 * HEAD), BF),
        pltpu.VMEM((2, SLOTS, WIDTH), F32),
        pltpu.VMEM((2, SLOTS, 2 * HEAD), F32),
        pltpu.VMEM((12, 8, 128), F32),
        pltpu.VMEM((2, SLOTS, WIDTH), F32),
        pltpu.VMEM((2, SLOTS, WIDTH), BF),
        pltpu.VMEM((2, SLOTS, WIDTH), BF),
        pltpu.VMEM((TENSOR, WIDTH, 2 * HEAD), BF),
    ]
    for _, cw in CHUNKS:
        n = cw // 4
        scratch += [
            pltpu.VMEM((2, 2 * cw, 2 * HEAD), BF),
            pltpu.VMEM((2 * cw, 2 * HEAD), BF),
            pltpu.VMEM((ZS, n, 2 * HEAD), BF),
            pltpu.VMEM((ZS - 1, n, 2 * HEAD), BF),
            pltpu.VMEM((n, 2 * HEAD), BF),
            pltpu.VMEM((n, 2 * HEAD), BF),
            pltpu.VMEM((4, 4, n, 2 * HEAD), BF),
        ]
    scratch += [pltpu.SemaphoreType.DMA((SEMS,)), pltpu.SemaphoreType.DMA((SEMS,)), pltpu.SemaphoreType.DMA((16,))]
    dq, ig, out = pl.pallas_call(
        kernel,
        name="layer_back",
        out_shape=(
            jax.ShapeDtypeStruct((2, SLOTS, WIDTH), BF),
            jax.ShapeDtypeStruct((2, SLOTS, WIDTH), BF),
            jax.ShapeDtypeStruct((TENSOR, WIDTH, 2 * HEAD), BF),
        ),
        in_specs=[any_spec] * 6 + [smem] * 5,
        out_specs=(any_spec,) * 3,
        scratch_shapes=scratch,
        compiler_params=pltpu.CompilerParams(
            collective_id=0, has_side_effects=True, vmem_limit_bytes=56 * 2**20
        ),
        cost_estimate=pl.CostEstimate(flops=6 * 10**9, bytes_accessed=16 * 10**6, transcendentals=15 * 10**5),
    )(
        layer_input.reshape(2, SLOTS, WIDTH),
        queries.reshape(2, SLOTS, WIDTH),
        projected_key_value.reshape(2, SLOTS, 2 * HEAD),
        output_grad.reshape(2, SLOTS, WIDTH),
        projection.reshape(TENSOR, WIDTH, 2 * HEAD),
        moment.reshape(TENSOR, WIDTH, 2 * HEAD),
        rewards,
        groups,
        lengths,
        assignment,
        sync_flags,
    )
    dq, ig, out = pl.pallas_call(
        place,
        name="place",
        out_shape=tuple(jax.ShapeDtypeStruct(a.shape, BF) for a in (dq, ig, out)),
        in_specs=[any_spec] * 3,
        out_specs=(any_spec,) * 3,
        scratch_shapes=[pltpu.VMEM(a.shape, BF) for a in (dq, ig, out)] + [pltpu.SemaphoreType.DMA((2, 12))],
    )(dq, ig, out)
    return (
        dq.reshape(2 * SLOTS, WIDTH),
        ig.reshape(2 * SLOTS, WIDTH),
        out.reshape(1, TENSOR * WIDTH, 1, 2 * HEAD),
    )


def solution(mesh):
    return jax.shard_map(
        shards,
        mesh=mesh,
        in_specs=(
            P("dp", "tensor"),
            P("dp", "tensor"),
            P("dp", "tensor", None),
            P("dp", "tensor"),
            P(None, "tensor", None),
            P("dp", None, "tensor", None),
            P("dp"),
            P("dp"),
            P(),
            P(),
            P(),
        ),
        out_specs=(P("dp", "tensor"), P("dp", "tensor"), P("dp", None, "tensor", None)),
        check_vma=False,
    )
```

```python
import functools
import math

import jax
import jax.numpy as jnp
from jax import lax
from jax.experimental import pallas as pl
from jax.experimental.pallas import tpu as pltpu
from jax.sharding import PartitionSpec as P

HEAD = 128
HEADS = 5
TENSOR = 8
ZS = 8
REPLICAS = 32
SLOTS = 384
WIDTH = 640
GROUP = 8
SYNCED = 4
CHUNKS = ((0, 384), (384, 256))
SEMS = 160
BF = jnp.bfloat16
F32 = jnp.float32
MESH = pl.DeviceIdType.MESH


def dot(a, b, ca, cb):
    return lax.dot_general(a, b, (((ca,), (cb,)), ((), ())), preferred_element_type=F32)


def kernel(*refs):
    nc = len(CHUNKS)
    refs = list(refs)
    take = lambda n: [refs.pop(0) for _ in range(n)]
    x_hbm, q_hbm, kv_hbm, do_hbm, proj_hbm, mom_hbm = take(6)
    rewards, groups, lengths, assignment, flags = take(5)
    dq_hbm, ig_hbm, mom_hbm_out = take(3)
    xv, qv, kvv, dov, pv, pg, mv, xg, xm, kvown, kvg, kva, kvm, st, dqf, dkv = take(16)
    rt, igf, dq_out, ig_out, mom_out = take(5)
    ar = [dict(zip(("sc", "cr", "ab", "zr", "xs", "xr", "mn"), take(7))) for _ in range(nc)]
    ss, rs, ls = take(3)

    dp = lax.axis_index("dp")
    t = lax.axis_index("tensor")
    xh, z, core = dp // 16, lax.rem(dp // 2, ZS), lax.rem(dp, 2)
    y, xl = t // 2, lax.rem(t, 2)

    def dev(xh_=xh, z_=z, core_=core, t_=t):
        return (xh_ * 16 + z_ * 2 + core_, t_)

    def ring(a, i, n):
        return lax.rem(a + (i + n), n)

    yt = lambda i, xl_=xl: ring(y, i, 4) * 2 + xl_
    pair_t = y * 2 + (1 - xl)
    pair = dev(t_=pair_t)
    yp, ym = dev(t_=yt(1)), dev(t_=yt(-1))
    sibling = dev(core_=1 - core)
    partner = dev(xh_=1 - xh)
    across = dev(xh_=1 - xh, t_=pair_t)
    tpeer = [dev(t_=ring(t, i, TENSOR)) for i in range(1, TENSOR)]
    zpeer = [dev(z_=ring(z, i, ZS)) for i in range(1, ZS)]

    counter = [0]
    sent = []

    def xfer(src, there, here, to):
        i = counter[0]
        counter[0] += 1
        copy = pltpu.make_async_remote_copy(src, there, ss.at[i], rs.at[i], device_id=to, device_id_type=MESH)
        copy.start()
        sent.append(copy)
        return pltpu.make_async_remote_copy(src, here, ss.at[i], rs.at[i], device_id=to, device_id_type=MESH)

    def local(src, dst, i):
        copy = pltpu.make_async_copy(src, dst, ls.at[i])
        copy.start()
        return copy

    lx = local(x_hbm, xv, 0)
    lproj = [local(proj_hbm.at[:, :, pl.ds(h * 128, 128)], pv.at[h], 1 + h) for h in range(2)]
    lkv = local(kv_hbm, kvv, 3)
    lq = local(q_hbm, qv, 4)
    ldo = local(do_hbm, dov, 5)
    lmom = local(mom_hbm, mv, 6)

    barrier = pltpu.get_barrier_semaphore()
    others = [sibling, partner, across] + tpeer + zpeer
    for other in others:
        pl.semaphore_signal(barrier, inc=1, device_id=other, device_id_type=MESH)

    moving = [assignment[2 * dp + j] != dp for j in range(2)]
    gone = jnp.where(moving[0], 0, 1)
    kept = 1 - gone

    group_row = lax.broadcasted_iota(jnp.int32, (8, 128), 0)
    tile = jnp.zeros((8, 128), F32)
    for j in range(2):
        tile = tile + jnp.where(group_row == groups[j], rewards[j], 0.0)
    rt[0] = tile

    lx.wait()
    xm[...] = xv[gone]
    xg[t, 0] = xv[kept]
    pl.semaphore_wait(barrier, len(others))

    HALF = SLOTS // 2
    top, low = pl.ds(0, HALF), pl.ds(HALF, HALF)

    def gather_kept(c0, cw):
        cols = pl.ds(c0, cw)
        at = lambda idx, rows=pl.ds(0, SLOTS): xg.at[idx, 0, rows, cols]
        own = at(t)
        a = xfer(own, own, at(pair_t), pair)
        b = xfer(own, own, at(yt(-1)), yp)
        c = xfer(own, own, at(yt(1)), ym)
        yield
        b.wait_recv()
        f = xfer(at(yt(-1), top), at(yt(-1), top), at(yt(2), top), yp)
        c.wait_recv()
        g = xfer(at(yt(1), low), at(yt(1), low), at(yt(2), low), ym)
        yield
        d = xfer(at(yt(-1)), at(yt(-1)), at(yt(-1, 1 - xl)), pair)
        e = xfer(at(yt(1)), at(yt(1)), at(yt(1, 1 - xl)), pair)
        yield
        f.wait_recv()
        g.wait_recv()
        h = xfer(at(yt(2)), at(yt(2)), at(yt(2, 1 - xl)), pair)
        yield
        for r in (a, d, e):
            r.wait_recv()
        yield
        h.wait_recv()

    def gather_moved(c0, cw):
        cols = pl.ds(c0, cw)
        at = lambda idx, rows=pl.ds(0, SLOTS): xg.at[idx, 1, rows, cols]
        a = xfer(xm.at[:, cols], at(t), at(pair_t), across)
        yield
        a.wait_recv()
        b = xfer(at(pair_t), at(pair_t), at(t), pair)
        up = [xfer(at(pair_t), at(pair_t), at(yt(-1, 1 - xl)), yp)]
        down = [xfer(at(pair_t), at(pair_t), at(yt(1, 1 - xl)), ym)]
        yield
        b.wait_recv()
        up.append(xfer(at(t), at(t), at(yt(-1)), yp))
        down.append(xfer(at(t), at(t), at(yt(1)), ym))
        last = []
        for i, x_ in ((0, 1 - xl), (1, xl)):
            yield
            up[i].wait_recv()
            p = at(yt(-1, x_), top)
            last.append(xfer(p, p, at(yt(2, x_), top), yp))
            down[i].wait_recv()
            p = at(yt(1, x_), low)
            last.append(xfer(p, p, at(yt(2, x_), low), ym))
        yield
        for r in last:
            r.wait_recv()

    SH = WIDTH // ZS

    def gather_projection():
        for cp in lproj:
            cp.wait()
        mine = pl.ds(pl.multiple_of(z * SH, 16), SH)
        pg[core, t, mine] = pv[core, t, mine]
        got = []
        for i in range(1, TENSOR):
            to = ring(t, i, TENSOR)
            frm = ring(t, -i, TENSOR)
            got.append(
                xfer(pv.at[core, to, mine], pg.at[core, t, mine], pg.at[core, frm, mine], tpeer[i - 1])
            )
        yield
        for r in got:
            r.wait_recv()
        got = []
        for i in range(1, ZS):
            theirs = pl.ds(pl.multiple_of(ring(z, -i, ZS) * SH, 16), SH)
            block = pg.at[core, :, mine]
            got.append(xfer(block, block, pg.at[core, :, theirs], zpeer[i - 1]))
        yield
        for r in got:
            r.wait_recv()
        a = xfer(pg.at[core], pg.at[core], pg.at[1 - core], sibling)
        yield
        a.wait_recv()

    def sum_rewards():
        a = xfer(rt.at[0], rt.at[1], rt.at[1], sibling)
        yield
        a.wait_recv()
        rt[2] = rt[0] + rt[1]
        got = [xfer(rt.at[2], rt.at[2 + i], rt.at[2 + i], zpeer[i - 1]) for i in range(1, ZS)]
        yield
        for r in got:
            r.wait_recv()
        total = rt[2]
        for i in range(1, ZS):
            total = total + rt[2 + i]
        rt[10] = total
        a = xfer(rt.at[10], rt.at[11], rt.at[11], partner)
        yield
        a.wait_recv()

    def attention(r):
        length = lengths[2 * dp + r]
        srow = lax.broadcasted_iota(jnp.int32, (SLOTS, SLOTS), 0)
        tcol = lax.broadcasted_iota(jnp.int32, (SLOTS, SLOTS), 1)
        allowed = (srow <= tcol) & (srow < length)
        live = lax.broadcasted_iota(jnp.int32, (SLOTS, HEAD), 0) < length
        scale = 1.0 / math.sqrt(HEAD)
        dkv[r] = jnp.zeros((SLOTS, 2 * HEAD), F32)

        @pl.loop(0, HEADS)
        def _(h):
            cols = pl.ds(pl.multiple_of(h * HEAD, HEAD), HEAD)
            q = qv[r, :, cols]
            g = jnp.where(live, dov[r, :, cols].astype(F32), 0.0).astype(BF)
            k = kvv[r, :, 0:HEAD]
            v = kvv[r, :, HEAD : 2 * HEAD]
            s = jnp.where(allowed, dot(k, q, 1, 1) * scale, -1e30)
            e = jnp.exp(s - jnp.max(s, axis=0, keepdims=True))
            att = e * (1.0 / jnp.sum(e, axis=0, keepdims=True))
            w = dot(v, g, 1, 1)
            delta = jnp.sum(att * w, axis=0, keepdims=True)
            ds = (att * (w - delta)).astype(BF)
            dkv[r, :, 0:HEAD] += dot(ds, q, 1, 0) * scale
            dkv[r, :, HEAD : 2 * HEAD] += dot(att.astype(BF), g, 1, 0)
            dqf[r, :, cols] = dot(ds, k, 0, 0) * scale

    def finish_attention():
        total = rt[10] + rt[11]
        for r in range(2):
            mean = jnp.sum(jnp.where(group_row == groups[r], total, 0.0), axis=0, keepdims=True)[:, 0:1] / GROUP
            advantage = rewards[r] - mean
            dq_out[r] = (dqf[r] * advantage).astype(BF)
            kvown[r] = (dkv[r] * advantage).astype(BF)
        kvg[t] = kvown[...]
        kva[0] = kvown[kept]
        kvm[...] = kvown[gone]

    def gather_key_values():
        at = lambda idx, r: kvg.at[idx, r]
        a = xfer(kvg.at[t], kvg.at[t], kvg.at[pair_t], pair)
        up = [xfer(kvg.at[t], kvg.at[t], kvg.at[yt(-1)], yp)]
        down = [xfer(kvg.at[t], kvg.at[t], kvg.at[yt(1)], ym)]
        yield
        a.wait_recv()
        up.append(xfer(kvg.at[pair_t], kvg.at[pair_t], kvg.at[yt(-1, 1 - xl)], yp))
        down.append(xfer(kvg.at[pair_t], kvg.at[pair_t], kvg.at[yt(1, 1 - xl)], ym))
        last = []
        for i, x_ in ((0, xl), (1, 1 - xl)):
            yield
            up[i].wait_recv()
            p = at(yt(-1, x_), 0)
            last.append(xfer(p, p, at(yt(2, x_), 0), yp))
            down[i].wait_recv()
            p = at(yt(1, x_), 1)
            last.append(xfer(p, p, at(yt(2, x_), 1), ym))
        yield
        for r in last:
            r.wait_recv()

    rank, where = [], [jnp.int32(0)] * SYNCED
    seen = jnp.int32(0)
    for j in range(TENSOR):
        on = flags[j] == 1
        rank.append(jnp.minimum(seen, SYNCED - 1))
        for k in range(SYNCED):
            where[k] = jnp.where(on & (seen == k), j, where[k])
        seen = seen + jnp.where(on, 1, 0)

    def new_state(c0, cw):
        @pl.loop(0, TENSOR)
        def _(b):
            grad = dot(xg[b, 0, :, c0 : c0 + cw], kva[0], 0, 0) + dot(xg[b, 1, :, c0 : c0 + cw], kva[1], 0, 0)
            st[b, c0 : c0 + cw] = (0.9 * mv[b, c0 : c0 + cw].astype(F32) + 0.1 * grad).astype(BF)

    def average(c0, cw, sc, cr, ab, zr, xs, xr, mn):
        n = cw // 4
        for k in range(SYNCED):
            sc[k // 2, (k % 2) * cw : (k % 2 + 1) * cw] = st[where[k], c0 : c0 + cw]
        a = xfer(sc.at[1 - core], cr, cr, sibling)
        yield
        a.wait_recv()
        for i in range(ZS):
            rows = slice(i * n, (i + 1) * n)
            ab[i] = (sc[core, rows].astype(F32) + cr[rows].astype(F32)).astype(BF)
        got = [xfer(ab.at[ring(z, i, ZS)], zr.at[i - 1], zr.at[i - 1], zpeer[i - 1]) for i in range(1, ZS)]
        yield
        total = ab[z].astype(F32)
        for i in range(1, ZS):
            got[i - 1].wait_recv()
            total = total + zr[i - 1].astype(F32)
        xs[...] = total.astype(BF)
        a = xfer(xs, xr, xr, partner)
        yield
        a.wait_recv()
        mine = mn.at[core * 2 + z // 4, lax.rem(z, 4)]
        mn[core * 2 + z // 4, lax.rem(z, 4)] = (
            (xs[...].astype(F32) + xr[...].astype(F32)) * (1.0 / REPLICAS)
        ).astype(BF)
        got = []
        for i in range(1, ZS):
            other = ring(z, -i, ZS)
            got.append(xfer(mine, mine, mn.at[core * 2 + other // 4, lax.rem(other, 4)], zpeer[i - 1]))
        yield
        for r in got:
            r.wait_recv()
        half = mn.at[pl.ds(core * 2, 2)]
        a = xfer(half, half, mn.at[pl.ds((1 - core) * 2, 2)], sibling)
        yield
        a.wait_recv()
        for j in range(TENSOR):
            synced = mn[rank[j]].reshape(cw, 2 * HEAD)
            mom_out[j, c0 : c0 + cw] = jnp.where(flags[j] == 1, synced, st[j, c0 : c0 + cw])

    def input_gradient(blocks, first, last):
        @pl.loop(0, 2)
        def _(r):
            total = None if first else igf[r]
            for b in blocks:
                weight = jnp.concatenate([pg[0, b], pg[1, b]], axis=1)
                term = dot(kvg[b, r], weight, 1, 1)
                total = term if total is None else total + term
            if last:
                ig_out[r] = total.astype(BF)
            else:
                igf[r] = total

    stores = []

    def store(src, dst):
        copy = pltpu.make_async_copy(src, dst, ls.at[7 + len(stores)])
        copy.start()
        stores.append(copy)

    def step(*generators):
        for g in generators:
            next(g, None)

    k0, k1 = [gather_kept(*c) for c in CHUNKS]
    m0, m1 = [gather_moved(*c) for c in CHUNKS]
    a0, a1 = [average(*c, **ar[i]) for i, c in enumerate(CHUNKS)]
    kvs = gather_key_values()
    pro, rew = gather_projection(), sum_rewards()
    step(m0, k0, m1, k1, rew, pro)
    lkv.wait()
    lq.wait()
    ldo.wait()
    attention(0)
    step(rew, pro)
    attention(1)
    step(rew)
    step(m0, m1, k0, k1)
    step(rew)
    finish_attention()
    store(dq_out, dq_hbm)
    swap = xfer(kvm, kva.at[1], kva.at[1], partner)
    step(m0, k0, m1, k0)
    step(m0, m0, m1, m1)
    step(k0)
    step(k1, k1)
    step(kvs)
    step(k0, m0)
    swap.wait_recv()
    lmom.wait()
    new_state(*CHUNKS[0])
    step(a0, a0)
    step(k1, k1, m1)
    new_state(*CHUNKS[1])
    step(a1, a0, a1)
    step(kvs, a0, pro, kvs, a1, a0, a1, kvs, pro)
    input_gradient((t, pair_t, yt(-1), yt(1), yt(-1, 1 - xl), yt(1, 1 - xl)), True, False)
    step(a0, a1)
    step(kvs)
    input_gradient((yt(2), yt(2, 1 - xl)), False, True)
    store(ig_out, ig_hbm)
    step(a1)
    store(mom_out, mom_hbm_out)
    for copy in stores:
        copy.wait()
    for copy in sent:
        copy.wait_send()


def place(dq, ig, out, dq_to, ig_to, out_to, dq_v, ig_v, out_v, sems):
    parts = [(a.at[r], v.at[r], b.at[r]) for a, v, b in ((dq, dq_v, dq_to), (ig, ig_v, ig_to)) for r in range(2)]
    parts += [(out.at[j], out_v.at[j], out_to.at[j]) for j in range(TENSOR)]
    loads = [pltpu.make_async_copy(a, v, sems.at[0, i]) for i, (a, v, _) in enumerate(parts)]
    stores = [pltpu.make_async_copy(v, b, sems.at[1, i]) for i, (_, v, b) in enumerate(parts)]
    for load in loads:
        load.start()
    for load, store in zip(loads, stores):
        load.wait()
        store.start()
    for store in stores:
        store.wait()


def shards(
    layer_input,
    queries,
    projected_key_value,
    output_grad,
    projection,
    moment,
    rewards,
    groups,
    lengths,
    assignment,
    sync_flags,
):
    any_spec = pl.BlockSpec(memory_space=pl.ANY)
    smem = pl.BlockSpec(memory_space=pltpu.SMEM)
    scratch = [
        pltpu.VMEM((2, SLOTS, WIDTH), BF),
        pltpu.VMEM((2, SLOTS, WIDTH), BF),
        pltpu.VMEM((2, SLOTS, 2 * HEAD), BF),
        pltpu.VMEM((2, SLOTS, WIDTH), BF),
        pltpu.VMEM((2, TENSOR, WIDTH, HEAD), BF),
        pltpu.VMEM((2, TENSOR, WIDTH, HEAD), BF),
        pltpu.VMEM((TENSOR, WIDTH, 2 * HEAD), BF),
        pltpu.VMEM((TENSOR, 2, SLOTS, WIDTH), BF),
        pltpu.VMEM((SLOTS, WIDTH), BF),
        pltpu.VMEM((2, SLOTS, 2 * HEAD), BF),
        pltpu.VMEM((TENSOR, 2, SLOTS, 2 * HEAD), BF),
        pltpu.VMEM((2, SLOTS, 2 * HEAD), BF),
        pltpu.VMEM((SLOTS, 2 * HEAD), BF),
        pltpu.VMEM((TENSOR, WIDTH, 2 * HEAD), BF),
        pltpu.VMEM((2, SLOTS, WIDTH), F32),
        pltpu.VMEM((2, SLOTS, 2 * HEAD), F32),
        pltpu.VMEM((12, 8, 128), F32),
        pltpu.VMEM((2, SLOTS, WIDTH), F32),
        pltpu.VMEM((2, SLOTS, WIDTH), BF),
        pltpu.VMEM((2, SLOTS, WIDTH), BF),
        pltpu.VMEM((TENSOR, WIDTH, 2 * HEAD), BF),
    ]
    for _, cw in CHUNKS:
        n = cw // 4
        scratch += [
            pltpu.VMEM((2, 2 * cw, 2 * HEAD), BF),
            pltpu.VMEM((2 * cw, 2 * HEAD), BF),
            pltpu.VMEM((ZS, n, 2 * HEAD), BF),
            pltpu.VMEM((ZS - 1, n, 2 * HEAD), BF),
            pltpu.VMEM((n, 2 * HEAD), BF),
            pltpu.VMEM((n, 2 * HEAD), BF),
            pltpu.VMEM((4, 4, n, 2 * HEAD), BF),
        ]
    scratch += [pltpu.SemaphoreType.DMA((SEMS,)), pltpu.SemaphoreType.DMA((SEMS,)), pltpu.SemaphoreType.DMA((16,))]
    dq, ig, out = pl.pallas_call(
        kernel,
        name="layer_back",
        out_shape=(
            jax.ShapeDtypeStruct((2, SLOTS, WIDTH), BF),
            jax.ShapeDtypeStruct((2, SLOTS, WIDTH), BF),
            jax.ShapeDtypeStruct((TENSOR, WIDTH, 2 * HEAD), BF),
        ),
        in_specs=[any_spec] * 6 + [smem] * 5,
        out_specs=(any_spec,) * 3,
        scratch_shapes=scratch,
        compiler_params=pltpu.CompilerParams(
            collective_id=0, has_side_effects=True, vmem_limit_bytes=56 * 2**20
        ),
        cost_estimate=pl.CostEstimate(flops=6 * 10**9, bytes_accessed=16 * 10**6, transcendentals=15 * 10**5),
    )(
        layer_input.reshape(2, SLOTS, WIDTH),
        queries.reshape(2, SLOTS, WIDTH),
        projected_key_value.reshape(2, SLOTS, 2 * HEAD),
        output_grad.reshape(2, SLOTS, WIDTH),
        projection.reshape(TENSOR, WIDTH, 2 * HEAD),
        moment.reshape(TENSOR, WIDTH, 2 * HEAD),
        rewards,
        groups,
        lengths,
        assignment,
        sync_flags,
    )
    dq, ig, out = pl.pallas_call(
        place,
        name="place",
        out_shape=tuple(jax.ShapeDtypeStruct(a.shape, BF) for a in (dq, ig, out)),
        in_specs=[any_spec] * 3,
        out_specs=(any_spec,) * 3,
        scratch_shapes=[pltpu.VMEM(a.shape, BF) for a in (dq, ig, out)] + [pltpu.SemaphoreType.DMA((2, 12))],
    )(dq, ig, out)
    return (
        dq.reshape(2 * SLOTS, WIDTH),
        ig.reshape(2 * SLOTS, WIDTH),
        out.reshape(1, TENSOR * WIDTH, 1, 2 * HEAD),
    )


def solution(mesh):
    return jax.shard_map(
        shards,
        mesh=mesh,
        in_specs=(
            P("dp", "tensor"),
            P("dp", "tensor"),
            P("dp", "tensor", None),
            P("dp", "tensor"),
            P(None, "tensor", None),
            P("dp", None, "tensor", None),
            P("dp"),
            P("dp"),
            P(),
            P(),
            P(),
        ),
        out_specs=(P("dp", "tensor"), P("dp", "tensor"), P("dp", None, "tensor", None)),
        check_vma=False,
    )
```
